32 devices in a mesh: ens: 2 (over y), lon: 4 (over z), lat: 4 (over x, core).
Axes of the slice: x: 2, y: 2, z: 4, core: 2. Of those that a mesh axis runs over, the one named last changes fastest.
Arguments:
- bed_depth: float32 [256, 4096], P('lat', 'lon'), may hold values from 0.5 to 2
- cotangent: float32 [512, 4096], P(('ens', 'lat'), 'lon'), parts along dimension 0, may hold values from -6 to 6
- sample_cell: int32 [131072], P(('lon', 'lat')), may hold values from 0 to 65535
- sample_owner: int32 [131072], P(('lon', 'lat')), may hold values from 0 to 15, as said below
- sample_reach: int32 [131072], P(('lon', 'lat')), may hold values from 0 to 1023
- sample_weight: float32 [131072], P(('lon', 'lat')), may hold values from 0.05 to 0.5
- sample_angle: float32 [131072], P(('lon', 'lat')), may hold values from -3.140625 to 3.140625
- sample_count: int32 [16], P(('lon', 'lat')), may hold values from 768 to 8192, as said below
- reach_width: float32 [16384], P(('lon', 'lat')), may hold values from 0.5 to 4
- reach_bed: float32 [16384], P(('lon', 'lat')), may hold values from 0.5 to 3
Outputs:
- grad_level: float32 [512, 4096], P(('ens', 'lat'), 'lon'), parts along dimension 0
- grad_width: float32 [32768], P(('ens', 'lon', 'lat')), parts along dimension 0
- grad_bed: float32 [32768], P(('ens', 'lon', 'lat')), parts along dimension 0
The draws below stay inside these ranges and needn't reach their ends.
There are 2 independent parts, one for each index of `ens`. The reference program is written for one: setup_inputs(seed, part) draws one part's arguments, and reference() takes and returns one part's arrays. A program takes and returns all parts, laid end to end along the dimension named above; an argument that names none is the same for every part. Nothing has to cross between parts.
Inputs may be any that keep to these rules, and one draw needn't show every extreme that they name: `sample_owner`: among the 8192 slots of one device at most 576 name any one owner, and in every draw one owner is named by exactly 576 live slots of every device. Slots 0 to sample_count - 1 of a device are live. Some device has all 8192 slots live.
All inputs are finite; a program needn't handle non-finite values.
Results may differ from the reference program's by a relative error of at most 0.0003.
Values sent between devices are 32-bit elements; how exact they have to be, the bound alone decides.
A program may use at most 192 MiB of HBM per device.

```python
import math
import jax
import jax.numpy as jnp

CLAT = 64
CLON = 1024
STEPS = 4
SAMP_DEV = 8192
REACH_DEV = 1024
OWNERS = 16
CAP = 576
NLAT = 256
NLON = 4096
SAMPLES = 131072
REACHES = 16384
N_LAT = 4


def device_counts(key):
    halve_key, jitter_key, full_key = jax.random.split(key, 3)
    halving = jax.random.randint(halve_key, (OWNERS,), 0, 4)
    ceiling = jnp.where(halving == 0, SAMP_DEV, jnp.where(halving == 1, SAMP_DEV // 2, jnp.where(halving == 2, SAMP_DEV // 4, SAMP_DEV // 8)))
    jitter = jax.random.randint(jitter_key, (OWNERS,), 0, 1 << 20) % (ceiling // 4 + 1)
    live_count = ceiling - jitter
    full_device = jax.random.randint(full_key, (), 0, OWNERS)
    return jnp.where(jnp.arange(OWNERS) == full_device, SAMP_DEV, live_count).astype(jnp.int32)


def draw_sample_count(key, part):
    live_counts = device_counts(key)
    return live_counts


def draw_sample_owner(key, part):
    live_counts = device_counts(key)
    key = jax.random.fold_in(key, 7)
    owner_key, device_key = jax.random.split(key, 2)
    full_owner = jax.random.randint(owner_key, (), 0, OWNERS)

    def one_device(slot_key, live_count):
        pool_key, shuffle_seed = jax.random.split(slot_key, 2)
        others = jnp.arange((OWNERS - 1) * CAP) // CAP
        others = others + (others >= full_owner).astype(others.dtype)
        others = jax.random.permutation(pool_key, others)
        owner_pool = jnp.concatenate([jnp.full((CAP,), full_owner, others.dtype), others])[:SAMP_DEV]
        positions = jnp.arange(SAMP_DEV)
        shuffle_key = jax.random.randint(shuffle_seed, (SAMP_DEV,), 0, SAMP_DEV) * SAMP_DEV + positions
        shuffle_key = jnp.where(positions < live_count, shuffle_key, SAMP_DEV * SAMP_DEV + positions)
        return owner_pool[jnp.argsort(shuffle_key)]
    device_keys = jax.random.split(device_key, OWNERS)
    return jax.vmap(one_device)(device_keys, live_counts).reshape(-1).astype(jnp.int32)


def draw_cotangent(key, part):
    key = jax.random.fold_in(key, 3)
    return jnp.clip(jax.random.normal(key, (NLAT, NLON), jnp.float32), -6.0, 6.0)


def place_ends(array, key, least, top_value):
    spot = [jax.random.randint(jax.random.fold_in(key, axis), (), 0, length) for axis, length in enumerate(array.shape)]
    widest = array.shape.index(max(array.shape))
    next_to = spot[:widest] + [(spot[widest] + 1) % array.shape[widest]] + spot[widest + 1:]
    return array.at[tuple(spot)].set(least).at[tuple(next_to)].set(top_value)


def block_levels(own_key, dims, cuts, least, high):
    def one(position, shards_of):
        steps = jax.random.uniform(jax.random.fold_in(jax.random.fold_in(own_key, 6), position), (shards_of,), jnp.float32, least / len(cuts), high / len(cuts))
        return jnp.repeat(jnp.exp(steps), dims[position] // shards_of).reshape((-1,) + (1,) * (len(dims) - position - 1))

    gain = one(*cuts[0])
    for cut in cuts[1:]:
        gain = gain * one(*cut)
    return gain


def setup_inputs(seed: int = 0, part: int = 0) -> dict:
    splits = jax.random.split(jax.random.key(seed), 11)
    part_splits = jax.random.split(jax.random.fold_in(splits[10], part), 11)
    bed_depth = jnp.clip(jnp.exp(math.log(2.0) - 1.3862944 * jax.random.uniform(splits[0], (NLAT, NLON), jnp.float32) ** block_levels(splits[0], (NLAT, NLON), ((0, 4), (1, 4)), -0.2, 0.2)), 0.5, 2.0)
    cotangent = draw_cotangent(jax.random.fold_in(jax.random.fold_in(splits[10], part), 71), part)
    sample_cell = place_ends(jax.random.randint(splits[2], (SAMPLES,), 0, CLAT * CLON), jax.random.fold_in(splits[2], 1), 0, (CLAT * CLON) - 1).astype(jnp.int32)
    sample_owner = draw_sample_owner(jax.random.fold_in(splits[10], 71), part)
    sample_reach = place_ends(jax.random.randint(splits[4], (SAMPLES,), 0, REACH_DEV), jax.random.fold_in(splits[4], 1), 0, REACH_DEV - 1).astype(jnp.int32)
    sample_weight = jnp.clip(jnp.exp(math.log(0.5) - 2.3025851 * jax.random.uniform(splits[5], (SAMPLES,), jnp.float32) ** block_levels(splits[5], (SAMPLES,), ((0, 16),), -0.2, 0.2)), 0.05, 0.5)
    sample_angle = jnp.clip(jax.random.uniform(splits[6], (SAMPLES,), jnp.float32, -3.140625, 3.140625), -3.140625, 3.140625)
    sample_count = draw_sample_count(jax.random.fold_in(splits[10], 71), part)
    reach_width = jnp.clip(jnp.exp(math.log(4.0) - 2.0794415 * jax.random.uniform(splits[8], (REACHES,), jnp.float32) ** block_levels(splits[8], (REACHES,), ((0, 16),), -0.2, 0.2)), 0.5, 4.0)
    reach_bed = jnp.clip(jnp.exp(math.log(3.0) - 1.7917595 * jax.random.uniform(splits[9], (REACHES,), jnp.float32) ** block_levels(splits[9], (REACHES,), ((0, 16),), -0.2, 0.2)), 0.5, 3.0)
    return {"bed_depth": bed_depth, "cotangent": cotangent, "sample_cell": sample_cell, "sample_owner": sample_owner, "sample_reach": sample_reach, "sample_weight": sample_weight, "sample_angle": sample_angle, "sample_count": sample_count, "reach_width": reach_width, "reach_bed": reach_bed}


WAVE_GAIN = 0.2
DRAG_RATE = 0.05


def coefficients(bed_field, north_ok):
    east_depth = 0.5 * (bed_field + jnp.roll(bed_field, -1, axis=1))
    north_depth = 0.5 * (bed_field + jnp.concatenate([bed_field[1:], bed_field[-1:]], axis=0))
    east_keep = 1.0 / (1.0 + DRAG_RATE / east_depth)
    north_keep = jnp.where(north_ok, 1.0 / (1.0 + DRAG_RATE / north_depth), 0.0)
    return east_keep, WAVE_GAIN * east_keep * east_depth, north_keep, WAVE_GAIN * north_keep * north_depth


def reference(bed_depth, cotangent, sample_cell, sample_owner, sample_reach, sample_weight, sample_angle, sample_count, reach_width, reach_bed):
    row_index = jnp.arange(NLAT)[:, None]
    north_ok = jnp.broadcast_to(row_index < NLAT - 1, (NLAT, NLON))
    east_keep, east_gain, north_keep, north_gain = coefficients(bed_depth, north_ok)
    blank_row = jnp.zeros((1, NLON), cotangent.dtype)
    level_adj = cotangent
    east_adj = jnp.zeros_like(cotangent)
    north_adj = jnp.zeros_like(cotangent)
    sum_level = jnp.zeros_like(cotangent)
    sum_east = jnp.zeros_like(cotangent)
    sum_north = jnp.zeros_like(cotangent)
    for step_index in range(STEPS):
        sum_level = sum_level + level_adj
        east_mid = east_adj + jnp.roll(level_adj, -1, axis=1) - level_adj
        north_level = jnp.concatenate([level_adj[1:], blank_row], axis=0)
        north_mid = jnp.where(north_ok, north_adj + north_level - level_adj, 0.0)
        east_flux = east_gain * east_mid
        north_flux = north_gain * north_mid
        south_flux = jnp.concatenate([blank_row, north_flux[:-1]], axis=0)
        level_adj = level_adj + east_flux - jnp.roll(east_flux, 1, axis=1) + north_flux - south_flux
        east_adj = east_keep * east_mid
        north_adj = north_keep * north_mid
        sum_east = sum_east + east_mid
        sum_north = sum_north + north_mid
    slot_index = jnp.arange(SAMPLES, dtype=jnp.int32)
    device_index = slot_index // SAMP_DEV
    live_slot = (slot_index % SAMP_DEV) < sample_count[device_index]
    grid_row = (device_index % N_LAT) * CLAT + sample_cell // CLON
    grid_col = (device_index // N_LAT) * CLON + sample_cell % CLON
    flat_cell = (grid_row * NLON + grid_col).astype(jnp.int32)
    sample_level = sum_level.reshape(-1)[flat_cell]
    sample_east = sum_east.reshape(-1)[flat_cell]
    sample_north = sum_north.reshape(-1)[flat_cell]
    level_term = jnp.where(live_slot, sample_weight * sample_level, 0.0)
    flow_term = jnp.where(live_slot, sample_weight * (jnp.cos(sample_angle) * sample_east + jnp.sin(sample_angle) * sample_north), 0.0)
    reach_index = (sample_owner * REACH_DEV + sample_reach).astype(jnp.int32)
    level_total = jax.ops.segment_sum(level_term, reach_index, num_segments=REACHES)
    flow_total = jax.ops.segment_sum(flow_term, reach_index, num_segments=REACHES)
    grad_width = reach_bed * level_total
    grad_bed = reach_width * level_total + reach_bed * flow_total
    return level_adj, grad_width, grad_bed
```

```python
import functools

import jax
import jax.numpy as jnp
from jax import lax
from jax.experimental import pallas as pl
from jax.experimental.pallas import tpu as pltpu
from jax.sharding import PartitionSpec as P

STEPS = 4
WAVE_GAIN = 0.2
DRAG_RATE = 0.05
MESH = pl.DeviceIdType.MESH
PAD_R = 8
PAD_C = 128
LANES = 128
GROUP = 8
TABLE = 256


def split(value):
    high = value.astype(jnp.bfloat16).astype(jnp.float32)
    return high, value - high


def kernel(
    dims,
    bed_ref,
    cot_ref,
    cell_ref,
    owner_ref,
    reach_ref,
    weight_ref,
    angle_ref,
    count_ref,
    width_ref,
    rbed_ref,
    level_out,
    gwidth_out,
    gbed_out,
    bed,
    lev,
    fields,
    hot,
    terms,
    spots,
    sums,
    recv,
    weights,
    halo_send,
    halo_recv,
    send_sem,
    recv_sem,
):
    n_lon, n_lat, rows, cols = dims
    owners = n_lon * n_lat
    lon, lat = lax.axis_index("lon"), lax.axis_index("lat")
    me = lon * n_lat + lat
    tall, wide = rows + 2 * PAD_R, cols + 2 * PAD_C
    slot_rows = cell_ref.shape[0]

    barrier = pltpu.get_barrier_semaphore()

    def peer(step):
        other = lax.rem(me + step, owners)
        return {"lon": other // n_lat, "lat": lax.rem(other, n_lat)}

    def greet(step, carry):
        pl.semaphore_signal(barrier, inc=1, device_id=peer(step), device_id_type=MESH)
        return carry

    lax.fori_loop(1, owners, greet, 0)
    lev[PAD_R : PAD_R + rows, PAD_C : PAD_C + cols] = cot_ref[...]
    bed[PAD_R : PAD_R + rows, PAD_C : PAD_C + cols] = bed_ref[...]
    pl.semaphore_wait(barrier, owners - 1)

    def span(step, length, pad):
        if step == 0:
            return pl.ds(0, length), pl.ds(pad, length)
        if step > 0:
            return pl.ds(length - pad, pad), pl.ds(0, pad)
        return pl.ds(0, pad), pl.ds(pad + length, pad)

    copies = []
    for d_lon, d_lat in ((1, 0), (-1, 0), (1, 1), (1, -1), (-1, 1), (-1, -1), (0, 1), (0, -1)):
        from_r, to_r = span(d_lat, rows, PAD_R)
        from_c, to_c = span(d_lon, cols, PAD_C)
        target = {
            "lon": lax.rem(lon + d_lon + n_lon, n_lon),
            "lat": lax.rem(lat + d_lat + n_lat, n_lat),
        }
        for source, place in ((bed_ref, bed), (cot_ref, lev)):
            index = len(copies)
            copy = pltpu.make_async_remote_copy(
                src_ref=source.at[from_r, from_c],
                dst_ref=place.at[to_r, to_c],
                send_sem=halo_send.at[index],
                recv_sem=halo_recv.at[index],
                device_id=target,
                device_id_type=MESH,
            )
            copy.start()
            copies.append(copy)

    slot = (
        lax.broadcasted_iota(jnp.int32, (slot_rows, LANES), 0) * LANES
        + lax.broadcasted_iota(jnp.int32, (slot_rows, LANES), 1)
    )
    weight = jnp.where(slot < count_ref[0], weight_ref[...], 0.0)
    angle = angle_ref[...]
    weights[0] = weight
    weights[1] = weight * jnp.cos(angle)
    weights[2] = weight * jnp.sin(angle)
    sums[...] = jnp.zeros_like(sums)

    for copy in copies:
        copy.wait()

    def east(value):
        return pltpu.roll(value, wide - 1, 1)

    def west(value):
        return pltpu.roll(value, 1, 1)

    def north(value):
        return pltpu.roll(value, tall - 1, 0)

    def south(value):
        return pltpu.roll(value, 1, 0)

    row = lat * rows - PAD_R + lax.broadcasted_iota(jnp.int32, (tall, wide), 0)
    open_north = (row >= 0) & (row < n_lat * rows - 1)
    depth = bed[...]
    east_depth = 0.5 * (depth + east(depth))
    north_depth = 0.5 * (depth + north(depth))
    east_keep = east_depth / (east_depth + DRAG_RATE)
    north_keep = jnp.where(open_north, north_depth / (north_depth + DRAG_RATE), 0.0)
    east_gain = WAVE_GAIN * east_keep * east_depth
    north_gain = WAVE_GAIN * north_keep * north_depth
    level = lev[...]
    sum_level = level
    for step in range(STEPS):
        east_mid = east(level) - level
        north_mid = north(level) - level
        if step > 0:
            sum_level = sum_level + level
            east_mid = east_mid + east_adj
            north_mid = north_mid + north_adj
        north_mid = jnp.where(open_north, north_mid, 0.0)
        east_flux = east_gain * east_mid
        north_flux = north_gain * north_mid
        level = level + east_flux - west(east_flux) + north_flux - south(north_flux)
        if step == 0:
            sum_east, sum_north = east_mid, north_mid
        else:
            sum_east, sum_north = sum_east + east_mid, sum_north + north_mid
        if step + 1 < STEPS:
            east_adj = east_keep * east_mid
            north_adj = north_keep * north_mid
    level_out[...] = level[PAD_R : PAD_R + rows, PAD_C : PAD_C + cols]

    half = cols // 2
    picks = 2 * rows
    for index, value in enumerate((sum_level, sum_east, sum_north)):
        for side in range(2):
            first = PAD_C + side * half
            high, low = split(value[PAD_R : PAD_R + rows, first : first + half])
            place = slice(index * picks + side * rows, index * picks + (side + 1) * rows)
            fields[place, 0:half] = high.astype(jnp.bfloat16)
            fields[place, half : 2 * half] = low.astype(jnp.bfloat16)

    reach_rows = width_ref.shape[0] // 2
    per_owner = 2 * reach_rows
    table = owners * per_owner
    block = GROUP * LANES

    def one_block(number, carry):
        here = pl.ds(pl.multiple_of(number * GROUP, GROUP), GROUP)
        cell = cell_ref[here, :]
        column = cell % cols
        deep = column % half
        pick = (column // half) * rows + cell // cols
        reach = reach_ref[here, :]
        tile = reach // LANES
        key = owner_ref[here, :] * reach_rows + tile % reach_rows
        lane = (tile // reach_rows) * LANES + reach % LANES
        for_level, for_east, for_north = (weights[i, here, :] for i in range(3))
        deep_ids = lax.broadcasted_iota(jnp.int32, (half, LANES), 0)
        pick_ids = lax.broadcasted_iota(jnp.int32, (picks, LANES), 0)
        lane_ids = lax.broadcasted_iota(jnp.int32, (TABLE, LANES), 0)
        line_ids = lax.broadcasted_iota(jnp.int32, (table, LANES), 0)
        key_ids = (line_ids // per_owner) * reach_rows + line_ids % reach_rows
        is_flow = (line_ids // reach_rows) % 2 == 1
        for i in range(GROUP):
            at = slice(i * LANES, (i + 1) * LANES)
            hot[:, at] = jnp.where(deep_ids == deep[i : i + 1], 1.0, 0.0).astype(jnp.bfloat16)
            spots[:, at] = jnp.where(lane_ids == lane[i : i + 1], 1.0, 0.0).astype(jnp.bfloat16)
        found = jnp.dot(
            fields[:, 0:half], hot[...], preferred_element_type=jnp.float32
        ) + jnp.dot(fields[:, half : 2 * half], hot[...], preferred_element_type=jnp.float32)
        for i in range(GROUP):
            at = slice(i * LANES, (i + 1) * LANES)
            mine = pick_ids == pick[i : i + 1]
            value = [
                jnp.sum(
                    jnp.where(mine, found[f * picks : (f + 1) * picks, at], 0.0),
                    axis=0,
                    keepdims=True,
                )
                for f in range(3)
            ]
            level_high, level_low = split(for_level[i : i + 1] * value[0])
            flow_high, flow_low = split(
                for_east[i : i + 1] * value[1] + for_north[i : i + 1] * value[2]
            )
            line = key_ids == key[i : i + 1]
            terms[0:table, at] = jnp.where(
                line, jnp.where(is_flow, flow_high, level_high), 0.0
            ).astype(jnp.bfloat16)
            terms[table : 2 * table, at] = jnp.where(
                line, jnp.where(is_flow, flow_low, level_low), 0.0
            ).astype(jnp.bfloat16)
        added = lax.dot_general(
            terms[...], spots[...], (((1,), (1,)), ((), ())), preferred_element_type=jnp.float32
        )
        sums[...] += added[0:table] + added[table : 2 * table]
        return carry

    lax.fori_loop(0, slot_rows * LANES // block, one_block, 0)

    def outgoing(step):
        other = lax.rem(me + step, owners)
        return pltpu.make_async_remote_copy(
            src_ref=sums.at[pl.ds(pl.multiple_of(other * per_owner, per_owner), per_owner)],
            dst_ref=recv.at[step],
            send_sem=send_sem.at[step],
            recv_sem=recv_sem.at[step],
            device_id=peer(step),
            device_id_type=MESH,
        )

    def send(step, carry):
        outgoing(step).start()
        return carry

    def take(step, total):
        outgoing(step).wait()
        return total + recv[step]

    lax.fori_loop(1, owners, send, 0)
    own = sums[pl.ds(pl.multiple_of(me * per_owner, per_owner), per_owner), :]
    total = lax.fori_loop(1, owners, take, own)
    level_total = jnp.concatenate(
        [total[0:reach_rows, 0:LANES], total[0:reach_rows, LANES:TABLE]], axis=0
    )
    flow_total = jnp.concatenate(
        [total[reach_rows:per_owner, 0:LANES], total[reach_rows:per_owner, LANES:TABLE]], axis=0
    )
    gwidth_out[...] = rbed_ref[...] * level_total
    gbed_out[...] = width_ref[...] * level_total + rbed_ref[...] * flow_total


def on_device(
    dims,
    bed_depth,
    cotangent,
    sample_cell,
    sample_owner,
    sample_reach,
    sample_weight,
    sample_angle,
    sample_count,
    reach_width,
    reach_bed,
):
    n_lon, n_lat = dims
    rows, cols = bed_depth.shape
    owners = n_lon * n_lat
    tall, wide = rows + 2 * PAD_R, cols + 2 * PAD_C
    slot_rows = sample_cell.shape[0] // LANES
    reach_tiles = reach_width.shape[0] // LANES
    per_owner = reach_tiles
    block = GROUP * LANES

    def tiled(value):
        return value.reshape(-1, LANES)

    vmem = pl.BlockSpec(memory_space=pltpu.VMEM)
    level, gwidth, gbed = pl.pallas_call(
        functools.partial(kernel, (n_lon, n_lat, rows, cols)),
        out_shape=(
            jax.ShapeDtypeStruct((rows, cols), jnp.float32),
            jax.ShapeDtypeStruct((reach_tiles, LANES), jnp.float32),
            jax.ShapeDtypeStruct((reach_tiles, LANES), jnp.float32),
        ),
        in_specs=[vmem] * 7 + [pl.BlockSpec(memory_space=pltpu.SMEM)] + [vmem] * 2,
        out_specs=(vmem, vmem, vmem),
        scratch_shapes=[
            pltpu.VMEM((tall, wide), jnp.float32),
            pltpu.VMEM((tall, wide), jnp.float32),
            pltpu.VMEM((6 * rows, cols), jnp.bfloat16),
            pltpu.VMEM((cols // 2, block), jnp.bfloat16),
            pltpu.VMEM((2 * owners * per_owner, block), jnp.bfloat16),
            pltpu.VMEM((TABLE, block), jnp.bfloat16),
            pltpu.VMEM((owners * per_owner, TABLE), jnp.float32),
            pltpu.VMEM((owners, per_owner, TABLE), jnp.float32),
            pltpu.VMEM((3, slot_rows, LANES), jnp.float32),
            pltpu.SemaphoreType.DMA((16,)),
            pltpu.SemaphoreType.DMA((16,)),
            pltpu.SemaphoreType.DMA((owners,)),
            pltpu.SemaphoreType.DMA((owners,)),
        ],
        compiler_params=pltpu.CompilerParams(
            collective_id=0, has_side_effects=True, vmem_limit_bytes=48 << 20
        ),
    )(
        bed_depth,
        cotangent,
        tiled(sample_cell),
        tiled(sample_owner),
        tiled(sample_reach),
        tiled(sample_weight),
        tiled(sample_angle),
        sample_count,
        tiled(reach_width),
        tiled(reach_bed),
    )
    return level, gwidth.reshape(-1), gbed.reshape(-1)


def solution(mesh):
    flat = P(("lon", "lat"))
    return jax.shard_map(
        functools.partial(on_device, (mesh.shape["lon"], mesh.shape["lat"])),
        mesh=mesh,
        in_specs=(P("lat", "lon"), P(("ens", "lat"), "lon")) + (flat,) * 8,
        out_specs=(P(("ens", "lat"), "lon"), P(("ens", "lon", "lat")), P(("ens", "lon", "lat"))),
        check_vma=False,
    )
```

```python
import functools

import jax
import jax.numpy as jnp
from jax import lax
from jax.experimental import pallas as pl
from jax.experimental.pallas import tpu as pltpu
from jax.sharding import PartitionSpec as P

STEPS = 4
WAVE_GAIN = 0.2
DRAG_RATE = 0.05
MESH = pl.DeviceIdType.MESH
PAD_R = 8
PAD_C = 128
LANES = 128
GROUP = 8
TABLE = 256


def split(value):
    high = value.astype(jnp.bfloat16).astype(jnp.float32)
    return high, value - high


def kernel(
    dims,
    bed_ref,
    cot_ref,
    cell_in,
    owner_in,
    reach_in,
    weight_in,
    angle_in,
    count_ref,
    width_in,
    rbed_in,
    level_out,
    gwidth_out,
    gbed_out,
    cell_ref,
    owner_ref,
    reach_ref,
    weight_ref,
    angle_ref,
    width_ref,
    rbed_ref,
    local_sem,
    bed,
    lev,
    fields,
    hot,
    found,
    terms,
    spots,
    sums,
    recv,
    weights,
    halo_send,
    halo_recv,
    send_sem,
    recv_sem,
):
    n_lon, n_lat, rows, cols = dims
    owners = n_lon * n_lat
    lon, lat = lax.axis_index("lon"), lax.axis_index("lat")
    me = lon * n_lat + lat
    tall, wide = rows + 2 * PAD_R, cols + 2 * PAD_C
    slot_rows = cell_ref.shape[0]

    barrier = pltpu.get_barrier_semaphore()

    def peer(step):
        other = lax.rem(me + step, owners)
        return {"lon": other // n_lat, "lat": lax.rem(other, n_lat)}

    def greet(step, carry):
        pl.semaphore_signal(barrier, inc=1, device_id=peer(step), device_id_type=MESH)
        return carry

    lax.fori_loop(1, owners, greet, 0)
    middle = (pl.ds(PAD_R, rows), pl.ds(PAD_C, cols))
    pairs = (
        (weight_in, weight_ref),
        (angle_in, angle_ref),
        (bed_ref, bed.at[middle]),
        (cot_ref, lev.at[middle]),
        (cell_in, cell_ref),
        (owner_in, owner_ref),
        (reach_in, reach_ref),
        (width_in, width_ref),
        (rbed_in, rbed_ref),
    )
    loads = [
        pltpu.make_async_copy(source, place, local_sem.at[i])
        for i, (source, place) in enumerate(pairs)
    ]
    for load in loads:
        load.start()
    pl.semaphore_wait(barrier, owners - 1)

    def span(step, length, pad):
        if step == 0:
            return pl.ds(0, length), pl.ds(pad, length)
        if step > 0:
            return pl.ds(length - pad, pad), pl.ds(0, pad)
        return pl.ds(0, pad), pl.ds(pad + length, pad)

    copies = []
    for d_lon, d_lat in ((1, 0), (-1, 0), (1, 1), (1, -1), (-1, 1), (-1, -1), (0, 1), (0, -1)):
        from_r, to_r = span(d_lat, rows, PAD_R)
        from_c, to_c = span(d_lon, cols, PAD_C)
        target = {
            "lon": lax.rem(lon + d_lon + n_lon, n_lon),
            "lat": lax.rem(lat + d_lat + n_lat, n_lat),
        }
        for source, place in ((bed_ref, bed), (cot_ref, lev)):
            index = len(copies)
            copy = pltpu.make_async_remote_copy(
                src_ref=source.at[from_r, from_c],
                dst_ref=place.at[to_r, to_c],
                send_sem=halo_send.at[index],
                recv_sem=halo_recv.at[index],
                device_id=target,
                device_id_type=MESH,
            )
            copy.start()
            copies.append(copy)

    for load in loads:
        load.wait()

    slot = (
        lax.broadcasted_iota(jnp.int32, (slot_rows, LANES), 0) * LANES
        + lax.broadcasted_iota(jnp.int32, (slot_rows, LANES), 1)
    )
    weight = jnp.where(slot < count_ref[0], weight_ref[...], 0.0)
    angle = angle_ref[...]
    weights[0] = weight
    weights[1] = weight * jnp.cos(angle)
    weights[2] = weight * jnp.sin(angle)
    sums[...] = jnp.zeros_like(sums)

    half = cols // 2
    picks = 2 * rows
    reach_rows = width_ref.shape[0] // 2
    per_owner = 2 * reach_rows
    table = owners * per_owner
    blocks = slot_rows // GROUP

    def mark(number, carry):
        here = pl.ds(pl.multiple_of(number * GROUP, GROUP), GROUP)
        deep = cell_ref[here, :] % half
        reach = reach_ref[here, :]
        lane = (reach // LANES // reach_rows) * LANES + reach % LANES
        deep_ids = lax.broadcasted_iota(jnp.int32, (half, LANES), 0)
        lane_ids = lax.broadcasted_iota(jnp.int32, (TABLE, LANES), 0)
        for i in range(GROUP):
            at = slice(i * LANES, (i + 1) * LANES)
            hot[number, :, at] = jnp.where(deep_ids == deep[i : i + 1], 1.0, 0.0).astype(
                jnp.bfloat16
            )
            spots[number, :, at] = jnp.where(lane_ids == lane[i : i + 1], 1.0, 0.0).astype(
                jnp.bfloat16
            )
        return carry

    lax.fori_loop(0, blocks, mark, 0)

    for copy in copies:
        copy.wait()

    def east(value):
        return pltpu.roll(value, wide - 1, 1)

    def west(value):
        return pltpu.roll(value, 1, 1)

    def north(value):
        return pltpu.roll(value, tall - 1, 0)

    def south(value):
        return pltpu.roll(value, 1, 0)

    row = lat * rows - PAD_R + lax.broadcasted_iota(jnp.int32, (tall, wide), 0)
    open_north = (row >= 0) & (row < n_lat * rows - 1)
    depth = bed[...]
    east_depth = 0.5 * (depth + east(depth))
    north_depth = 0.5 * (depth + north(depth))
    east_keep = east_depth / (east_depth + DRAG_RATE)
    north_keep = jnp.where(open_north, north_depth / (north_depth + DRAG_RATE), 0.0)
    east_gain = WAVE_GAIN * east_keep * east_depth
    north_gain = WAVE_GAIN * north_keep * north_depth
    level = lev[...]
    sum_level = level
    for step in range(STEPS):
        east_mid = east(level) - level
        north_mid = north(level) - level
        if step > 0:
            sum_level = sum_level + level
            east_mid = east_mid + east_adj
            north_mid = north_mid + north_adj
        north_mid = jnp.where(open_north, north_mid, 0.0)
        east_flux = east_gain * east_mid
        north_flux = north_gain * north_mid
        level = level + east_flux - west(east_flux) + north_flux - south(north_flux)
        if step == 0:
            sum_east, sum_north = east_mid, north_mid
        else:
            sum_east, sum_north = sum_east + east_mid, sum_north + north_mid
        if step + 1 < STEPS:
            east_adj = east_keep * east_mid
            north_adj = north_keep * north_mid
    level_out[...] = level[PAD_R : PAD_R + rows, PAD_C : PAD_C + cols]

    for index, value in enumerate((sum_level, sum_east, sum_north)):
        for side in range(2):
            first = PAD_C + side * half
            high, low = split(value[PAD_R : PAD_R + rows, first : first + half])
            place = slice(index * picks + side * rows, index * picks + (side + 1) * rows)
            fields[place, 0:half] = high.astype(jnp.bfloat16)
            fields[place, half : 2 * half] = low.astype(jnp.bfloat16)

    def found_in(number):
        here = hot[number]
        return jnp.dot(
            fields[:, 0:half], here, preferred_element_type=jnp.float32
        ) + jnp.dot(fields[:, half : 2 * half], here, preferred_element_type=jnp.float32)

    def add_terms(number, side):
        here = pl.ds(pl.multiple_of(number * GROUP, GROUP), GROUP)
        cell = cell_ref[here, :]
        pick = ((cell % cols) // half) * rows + cell // cols
        key = owner_ref[here, :] * reach_rows + (reach_ref[here, :] // LANES) % reach_rows
        for_level, for_east, for_north = (weights[i, here, :] for i in range(3))
        pick_ids = lax.broadcasted_iota(jnp.int32, (picks, LANES), 0)
        line_ids = lax.broadcasted_iota(jnp.int32, (table, LANES), 0)
        key_ids = (line_ids // per_owner) * reach_rows + line_ids % reach_rows
        is_flow = (line_ids // reach_rows) % 2 == 1
        for i in range(GROUP):
            at = slice(i * LANES, (i + 1) * LANES)
            mine = pick_ids == pick[i : i + 1]
            value = [
                jnp.sum(
                    jnp.where(mine, found[side, f * picks : (f + 1) * picks, at], 0.0),
                    axis=0,
                    keepdims=True,
                )
                for f in range(3)
            ]
            level_high, level_low = split(for_level[i : i + 1] * value[0])
            flow_high, flow_low = split(
                for_east[i : i + 1] * value[1] + for_north[i : i + 1] * value[2]
            )
            line = key_ids == key[i : i + 1]
            terms[side, 0:table, at] = jnp.where(
                line, jnp.where(is_flow, flow_high, level_high), 0.0
            ).astype(jnp.bfloat16)
            terms[side, table : 2 * table, at] = jnp.where(
                line, jnp.where(is_flow, flow_low, level_low), 0.0
            ).astype(jnp.bfloat16)
        added = lax.dot_general(
            terms[side],
            spots[number],
            (((1,), (1,)), ((), ())),
            preferred_element_type=jnp.float32,
        )
        sums[...] += added[0:table] + added[table : 2 * table]

    found[0] = found_in(0)

    def two_blocks(pair, carry):
        for side in range(2):
            found[1 - side] = found_in(2 * pair + side + 1)
            add_terms(2 * pair + side, side)
        return carry

    lax.fori_loop(0, blocks // 2 - 1, two_blocks, 0)
    found[1] = found_in(blocks - 1)
    add_terms(blocks - 2, 0)
    add_terms(blocks - 1, 1)

    def outgoing(step):
        other = lax.rem(me + step, owners)
        return pltpu.make_async_remote_copy(
            src_ref=sums.at[pl.ds(pl.multiple_of(other * per_owner, per_owner), per_owner)],
            dst_ref=recv.at[step],
            send_sem=send_sem.at[step],
            recv_sem=recv_sem.at[step],
            device_id=peer(step),
            device_id_type=MESH,
        )

    def send(step, carry):
        outgoing(step).start()
        return carry

    def take(step, total):
        outgoing(step).wait()
        return total + recv[step]

    lax.fori_loop(1, owners, send, 0)
    own = sums[pl.ds(pl.multiple_of(me * per_owner, per_owner), per_owner), :]
    total = lax.fori_loop(1, owners, take, own)
    level_total = jnp.concatenate(
        [total[0:reach_rows, 0:LANES], total[0:reach_rows, LANES:TABLE]], axis=0
    )
    flow_total = jnp.concatenate(
        [total[reach_rows:per_owner, 0:LANES], total[reach_rows:per_owner, LANES:TABLE]], axis=0
    )
    gwidth_out[...] = rbed_ref[...] * level_total
    gbed_out[...] = width_ref[...] * level_total + rbed_ref[...] * flow_total


def on_device(
    dims,
    bed_depth,
    cotangent,
    sample_cell,
    sample_owner,
    sample_reach,
    sample_weight,
    sample_angle,
    sample_count,
    reach_width,
    reach_bed,
):
    n_lon, n_lat = dims
    rows, cols = bed_depth.shape
    owners = n_lon * n_lat
    tall, wide = rows + 2 * PAD_R, cols + 2 * PAD_C
    slot_rows = sample_cell.shape[0] // LANES
    reach_tiles = reach_width.shape[0] // LANES
    per_owner = reach_tiles
    block = GROUP * LANES
    blocks = slot_rows // GROUP

    def tiled(value):
        return value.reshape(-1, LANES)

    hbm = pl.BlockSpec(memory_space=pltpu.HBM)
    vmem = pl.BlockSpec(memory_space=pltpu.VMEM)
    level, gwidth, gbed = pl.pallas_call(
        functools.partial(kernel, (n_lon, n_lat, rows, cols)),
        out_shape=(
            jax.ShapeDtypeStruct((rows, cols), jnp.float32),
            jax.ShapeDtypeStruct((reach_tiles, LANES), jnp.float32),
            jax.ShapeDtypeStruct((reach_tiles, LANES), jnp.float32),
        ),
        in_specs=[hbm] * 7 + [pl.BlockSpec(memory_space=pltpu.SMEM)] + [hbm] * 2,
        out_specs=(vmem, vmem, vmem),
        scratch_shapes=[
            pltpu.VMEM((slot_rows, LANES), jnp.int32),
            pltpu.VMEM((slot_rows, LANES), jnp.int32),
            pltpu.VMEM((slot_rows, LANES), jnp.int32),
            pltpu.VMEM((slot_rows, LANES), jnp.float32),
            pltpu.VMEM((slot_rows, LANES), jnp.float32),
            pltpu.VMEM((reach_tiles, LANES), jnp.float32),
            pltpu.VMEM((reach_tiles, LANES), jnp.float32),
            pltpu.SemaphoreType.DMA((9,)),
            pltpu.VMEM((tall, wide), jnp.float32),
            pltpu.VMEM((tall, wide), jnp.float32),
            pltpu.VMEM((6 * rows, cols), jnp.bfloat16),
            pltpu.VMEM((blocks, cols // 2, block), jnp.bfloat16),
            pltpu.VMEM((2, 6 * rows, block), jnp.float32),
            pltpu.VMEM((2, 2 * owners * per_owner, block), jnp.bfloat16),
            pltpu.VMEM((blocks, TABLE, block), jnp.bfloat16),
            pltpu.VMEM((owners * per_owner, TABLE), jnp.float32),
            pltpu.VMEM((owners, per_owner, TABLE), jnp.float32),
            pltpu.VMEM((3, slot_rows, LANES), jnp.float32),
            pltpu.SemaphoreType.DMA((16,)),
            pltpu.SemaphoreType.DMA((16,)),
            pltpu.SemaphoreType.DMA((owners,)),
            pltpu.SemaphoreType.DMA((owners,)),
        ],
        compiler_params=pltpu.CompilerParams(
            collective_id=0, has_side_effects=True, vmem_limit_bytes=63 << 20
        ),
    )(
        bed_depth,
        cotangent,
        tiled(sample_cell),
        tiled(sample_owner),
        tiled(sample_reach),
        tiled(sample_weight),
        tiled(sample_angle),
        sample_count,
        tiled(reach_width),
        tiled(reach_bed),
    )
    return level, gwidth.reshape(-1), gbed.reshape(-1)


def solution(mesh):
    flat = P(("lon", "lat"))
    return jax.shard_map(
        functools.partial(on_device, (mesh.shape["lon"], mesh.shape["lat"])),
        mesh=mesh,
        in_specs=(P("lat", "lon"), P(("ens", "lat"), "lon")) + (flat,) * 8,
        out_specs=(P(("ens", "lat"), "lon"), P(("ens", "lon", "lat")), P(("ens", "lon", "lat"))),
        check_vma=False,
    )
```

```python
import functools

import jax
import jax.numpy as jnp
from jax import lax
from jax.experimental import pallas as pl
from jax.experimental.pallas import tpu as pltpu
from jax.sharding import PartitionSpec as P

STEPS = 4
WAVE_GAIN = 0.2
DRAG_RATE = 0.05
MESH = pl.DeviceIdType.MESH
PAD_R = 8
PAD_C = 128
LANES = 128
GROUP = 8
TABLE = 256


def split(value):
    high = value.astype(jnp.bfloat16).astype(jnp.float32)
    return high, value - high


def kernel(
    dims,
    bed_ref,
    cot_ref,
    cell_in,
    owner_in,
    reach_in,
    weight_in,
    angle_in,
    count_ref,
    width_in,
    rbed_in,
    level_out,
    gwidth_out,
    gbed_out,
    cell_ref,
    owner_ref,
    reach_ref,
    weight_ref,
    angle_ref,
    width_ref,
    rbed_ref,
    local_sem,
    bed,
    lev,
    fields,
    hot,
    found,
    terms,
    spots,
    sums,
    recv,
    weights,
    halo_send,
    halo_recv,
    send_sem,
    recv_sem,
):
    n_lon, n_lat, rows, cols = dims
    owners = n_lon * n_lat
    lon, lat = lax.axis_index("lon"), lax.axis_index("lat")
    me = lon * n_lat + lat
    tall, wide = rows + 2 * PAD_R, cols + 2 * PAD_C
    slot_rows = cell_ref.shape[0]

    barrier = pltpu.get_barrier_semaphore()

    def peer(step):
        other = lax.rem(me + step, owners)
        return {"lon": other // n_lat, "lat": lax.rem(other, n_lat)}

    def greet(step, carry):
        pl.semaphore_signal(barrier, inc=1, device_id=peer(step), device_id_type=MESH)
        return carry

    lax.fori_loop(1, owners, greet, 0)
    middle = (pl.ds(PAD_R, rows), pl.ds(PAD_C, cols))
    pairs = (
        (weight_in, weight_ref),
        (angle_in, angle_ref),
        (bed_ref, bed.at[middle]),
        (cot_ref, lev.at[middle]),
        (cell_in, cell_ref),
        (owner_in, owner_ref),
        (reach_in, reach_ref),
        (width_in, width_ref),
        (rbed_in, rbed_ref),
    )
    loads = [
        pltpu.make_async_copy(source, place, local_sem.at[i])
        for i, (source, place) in enumerate(pairs)
    ]
    for load in loads:
        load.start()
    pl.semaphore_wait(barrier, owners - 1)

    def span(step, length, pad):
        if step == 0:
            return pl.ds(0, length), pl.ds(pad, length)
        if step > 0:
            return pl.ds(length - pad, pad), pl.ds(0, pad)
        return pl.ds(0, pad), pl.ds(pad + length, pad)

    copies = []
    for d_lon, d_lat in ((1, 0), (-1, 0), (1, 1), (1, -1), (-1, 1), (-1, -1), (0, 1), (0, -1)):
        from_r, to_r = span(d_lat, rows, PAD_R)
        from_c, to_c = span(d_lon, cols, PAD_C)
        target = {
            "lon": lax.rem(lon + d_lon + n_lon, n_lon),
            "lat": lax.rem(lat + d_lat + n_lat, n_lat),
        }
        for source, place in ((bed_ref, bed), (cot_ref, lev)):
            index = len(copies)
            copy = pltpu.make_async_remote_copy(
                src_ref=source.at[from_r, from_c],
                dst_ref=place.at[to_r, to_c],
                send_sem=halo_send.at[index],
                recv_sem=halo_recv.at[index],
                device_id=target,
                device_id_type=MESH,
            )
            copy.start()
            copies.append(copy)

    for load in loads:
        load.wait()

    slot = (
        lax.broadcasted_iota(jnp.int32, (slot_rows, LANES), 0) * LANES
        + lax.broadcasted_iota(jnp.int32, (slot_rows, LANES), 1)
    )
    weight = jnp.where(slot < count_ref[0], weight_ref[...], 0.0)
    angle = angle_ref[...]
    weights[0] = weight
    weights[1] = weight * jnp.cos(angle)
    weights[2] = weight * jnp.sin(angle)
    sums[...] = jnp.zeros_like(sums)

    half = cols // 2
    picks = 2 * rows
    reach_rows = width_ref.shape[0] // 2
    per_owner = 2 * reach_rows
    table = owners * per_owner
    blocks = slot_rows // GROUP

    def mark(number, carry):
        here = pl.ds(pl.multiple_of(number * GROUP, GROUP), GROUP)
        deep = cell_ref[here, :] % half
        reach = reach_ref[here, :]
        lane = (reach // LANES // reach_rows) * LANES + reach % LANES
        deep_ids = lax.broadcasted_iota(jnp.int32, (half, LANES), 0)
        lane_ids = lax.broadcasted_iota(jnp.int32, (TABLE, LANES), 0)
        for i in range(GROUP):
            at = slice(i * LANES, (i + 1) * LANES)
            hot[number, :, at] = jnp.where(deep_ids == deep[i : i + 1], 1.0, 0.0).astype(
                jnp.bfloat16
            )
            spots[number, :, at] = jnp.where(lane_ids == lane[i : i + 1], 1.0, 0.0).astype(
                jnp.bfloat16
            )
        return carry

    lax.fori_loop(0, blocks, mark, 0)

    for copy in copies:
        copy.wait()

    def east(value):
        return pltpu.roll(value, wide - 1, 1)

    def west(value):
        return pltpu.roll(value, 1, 1)

    def north(value):
        return pltpu.roll(value, tall - 1, 0)

    def south(value):
        return pltpu.roll(value, 1, 0)

    row = lat * rows - PAD_R + lax.broadcasted_iota(jnp.int32, (tall, wide), 0)
    open_north = (row >= 0) & (row < n_lat * rows - 1)
    depth = bed[...]
    east_depth = 0.5 * (depth + east(depth))
    north_depth = 0.5 * (depth + north(depth))
    east_keep = east_depth / (east_depth + DRAG_RATE)
    north_keep = jnp.where(open_north, north_depth / (north_depth + DRAG_RATE), 0.0)
    east_gain = WAVE_GAIN * east_keep * east_depth
    north_gain = WAVE_GAIN * north_keep * north_depth
    level = lev[...]
    sum_level = level
    for step in range(STEPS):
        east_mid = east(level) - level
        north_mid = north(level) - level
        if step > 0:
            sum_level = sum_level + level
            east_mid = east_mid + east_adj
            north_mid = north_mid + north_adj
        north_mid = jnp.where(open_north, north_mid, 0.0)
        east_flux = east_gain * east_mid
        north_flux = north_gain * north_mid
        level = level + east_flux - west(east_flux) + north_flux - south(north_flux)
        if step == 0:
            sum_east, sum_north = east_mid, north_mid
        else:
            sum_east, sum_north = sum_east + east_mid, sum_north + north_mid
        if step + 1 < STEPS:
            east_adj = east_keep * east_mid
            north_adj = north_keep * north_mid
    level_out[...] = level[PAD_R : PAD_R + rows, PAD_C : PAD_C + cols]

    for index, value in enumerate((sum_level, sum_east, sum_north)):
        for side in range(2):
            first = PAD_C + side * half
            high, low = split(value[PAD_R : PAD_R + rows, first : first + half])
            place = slice(index * picks + side * rows, index * picks + (side + 1) * rows)
            fields[place, 0:half] = high.astype(jnp.bfloat16)
            fields[place, half : 2 * half] = low.astype(jnp.bfloat16)

    def found_in(number):
        here = hot[number]
        return jnp.dot(
            fields[:, 0:half], here, preferred_element_type=jnp.float32
        ) + jnp.dot(fields[:, half : 2 * half], here, preferred_element_type=jnp.float32)

    def add_terms(number, side):
        here = pl.ds(pl.multiple_of(number * GROUP, GROUP), GROUP)
        cell = cell_ref[here, :]
        pick = ((cell % cols) // half) * rows + cell // cols
        key = owner_ref[here, :] * reach_rows + (reach_ref[here, :] // LANES) % reach_rows
        for_level, for_east, for_north = (weights[i, here, :] for i in range(3))
        pick_ids = lax.broadcasted_iota(jnp.int32, (picks, LANES), 0)
        line_ids = lax.broadcasted_iota(jnp.int32, (table, LANES), 0)
        key_ids = (line_ids // per_owner) * reach_rows + line_ids % reach_rows
        is_flow = (line_ids // reach_rows) % 2 == 1
        for i in range(GROUP):
            at = slice(i * LANES, (i + 1) * LANES)
            mine = pick_ids == pick[i : i + 1]
            value = [
                jnp.sum(
                    jnp.where(mine, found[side, f * picks : (f + 1) * picks, at], 0.0),
                    axis=0,
                    keepdims=True,
                )
                for f in range(3)
            ]
            level_high, level_low = split(for_level[i : i + 1] * value[0])
            flow_high, flow_low = split(
                for_east[i : i + 1] * value[1] + for_north[i : i + 1] * value[2]
            )
            line = key_ids == key[i : i + 1]
            terms[side, 0:table, at] = jnp.where(
                line, jnp.where(is_flow, flow_high, level_high), 0.0
            ).astype(jnp.bfloat16)
            terms[side, table : 2 * table, at] = jnp.where(
                line, jnp.where(is_flow, flow_low, level_low), 0.0
            ).astype(jnp.bfloat16)
        added = lax.dot_general(
            terms[side],
            spots[number],
            (((1,), (1,)), ((), ())),
            preferred_element_type=jnp.float32,
        )
        sums[...] += added[0:table] + added[table : 2 * table]

    found[0] = found_in(0)

    def two_blocks(pair, carry):
        for side in range(2):
            found[1 - side] = found_in(2 * pair + side + 1)
            add_terms(2 * pair + side, side)
        return carry

    lax.fori_loop(0, blocks // 2 - 1, two_blocks, 0)
    found[1] = found_in(blocks - 1)
    add_terms(blocks - 2, 0)
    add_terms(blocks - 1, 1)

    def outgoing(step):
        other = lax.rem(me + step, owners)
        return pltpu.make_async_remote_copy(
            src_ref=sums.at[pl.ds(pl.multiple_of(other * per_owner, per_owner), per_owner)],
            dst_ref=recv.at[step],
            send_sem=send_sem.at[step],
            recv_sem=recv_sem.at[step],
            device_id=peer(step),
            device_id_type=MESH,
        )

    def send(step, carry):
        outgoing(step).start()
        return carry

    def take(step, total):
        outgoing(step).wait()
        return total + recv[step]

    lax.fori_loop(1, owners, send, 0)
    own = sums[pl.ds(pl.multiple_of(me * per_owner, per_owner), per_owner), :]
    total = lax.fori_loop(1, owners, take, own)
    level_total = jnp.concatenate(
        [total[0:reach_rows, 0:LANES], total[0:reach_rows, LANES:TABLE]], axis=0
    )
    flow_total = jnp.concatenate(
        [total[reach_rows:per_owner, 0:LANES], total[reach_rows:per_owner, LANES:TABLE]], axis=0
    )
    gwidth_out[...] = rbed_ref[...] * level_total
    gbed_out[...] = width_ref[...] * level_total + rbed_ref[...] * flow_total


def on_device(
    dims,
    bed_depth,
    cotangent,
    sample_cell,
    sample_owner,
    sample_reach,
    sample_weight,
    sample_angle,
    sample_count,
    reach_width,
    reach_bed,
):
    n_lon, n_lat = dims
    rows, cols = bed_depth.shape
    owners = n_lon * n_lat
    tall, wide = rows + 2 * PAD_R, cols + 2 * PAD_C
    slot_rows = sample_cell.shape[0] // LANES
    reach_tiles = reach_width.shape[0] // LANES
    per_owner = reach_tiles
    block = GROUP * LANES
    blocks = slot_rows // GROUP

    def tiled(value):
        return value.reshape(-1, LANES)

    hbm = pl.BlockSpec(memory_space=pltpu.HBM)
    def in_hbm(value):
        return pltpu.with_memory_space_constraint(value, pltpu.HBM)

    vmem = pl.BlockSpec(memory_space=pltpu.VMEM)
    level, gwidth, gbed = pl.pallas_call(
        functools.partial(kernel, (n_lon, n_lat, rows, cols)),
        out_shape=(
            jax.ShapeDtypeStruct((rows, cols), jnp.float32),
            jax.ShapeDtypeStruct((reach_tiles, LANES), jnp.float32),
            jax.ShapeDtypeStruct((reach_tiles, LANES), jnp.float32),
        ),
        in_specs=[hbm] * 7 + [pl.BlockSpec(memory_space=pltpu.SMEM)] + [hbm] * 2,
        out_specs=(vmem, vmem, vmem),
        scratch_shapes=[
            pltpu.VMEM((slot_rows, LANES), jnp.int32),
            pltpu.VMEM((slot_rows, LANES), jnp.int32),
            pltpu.VMEM((slot_rows, LANES), jnp.int32),
            pltpu.VMEM((slot_rows, LANES), jnp.float32),
            pltpu.VMEM((slot_rows, LANES), jnp.float32),
            pltpu.VMEM((reach_tiles, LANES), jnp.float32),
            pltpu.VMEM((reach_tiles, LANES), jnp.float32),
            pltpu.SemaphoreType.DMA((9,)),
            pltpu.VMEM((tall, wide), jnp.float32),
            pltpu.VMEM((tall, wide), jnp.float32),
            pltpu.VMEM((6 * rows, cols), jnp.bfloat16),
            pltpu.VMEM((blocks, cols // 2, block), jnp.bfloat16),
            pltpu.VMEM((2, 6 * rows, block), jnp.float32),
            pltpu.VMEM((2, 2 * owners * per_owner, block), jnp.bfloat16),
            pltpu.VMEM((blocks, TABLE, block), jnp.bfloat16),
            pltpu.VMEM((owners * per_owner, TABLE), jnp.float32),
            pltpu.VMEM((owners, per_owner, TABLE), jnp.float32),
            pltpu.VMEM((3, slot_rows, LANES), jnp.float32),
            pltpu.SemaphoreType.DMA((16,)),
            pltpu.SemaphoreType.DMA((16,)),
            pltpu.SemaphoreType.DMA((owners,)),
            pltpu.SemaphoreType.DMA((owners,)),
        ],
        compiler_params=pltpu.CompilerParams(
            collective_id=0, has_side_effects=True, vmem_limit_bytes=48 << 20
        ),
    )(
        in_hbm(bed_depth),
        in_hbm(cotangent),
        in_hbm(tiled(sample_cell)),
        in_hbm(tiled(sample_owner)),
        in_hbm(tiled(sample_reach)),
        in_hbm(tiled(sample_weight)),
        in_hbm(tiled(sample_angle)),
        sample_count,
        in_hbm(tiled(reach_width)),
        in_hbm(tiled(reach_bed)),
    )
    return level, gwidth.reshape(-1), gbed.reshape(-1)


def solution(mesh):
    flat = P(("lon", "lat"))
    return jax.shard_map(
        functools.partial(on_device, (mesh.shape["lon"], mesh.shape["lat"])),
        mesh=mesh,
        in_specs=(P("lat", "lon"), P(("ens", "lat"), "lon")) + (flat,) * 8,
        out_specs=(P(("ens", "lat"), "lon"), P(("ens", "lon", "lat")), P(("ens", "lon", "lat"))),
        check_vma=False,
    )
```

```python
import functools

import jax
import jax.numpy as jnp
from jax import lax
from jax.experimental import pallas as pl
from jax.experimental.pallas import tpu as pltpu
from jax.sharding import PartitionSpec as P

STEPS = 4
WAVE_GAIN = 0.2
DRAG_RATE = 0.05
MESH = pl.DeviceIdType.MESH
PAD_R = 8
PAD_C = 128
LANES = 128
GROUP = 8
TABLE = 256


def split(value):
    high = value.astype(jnp.bfloat16).astype(jnp.float32)
    return high, value - high


def kernel(
    dims,
    bed_ref,
    cot_ref,
    cell_in,
    owner_in,
    reach_in,
    weight_in,
    angle_in,
    count_ref,
    width_in,
    rbed_in,
    level_out,
    gwidth_out,
    gbed_out,
    cell_ref,
    owner_ref,
    reach_ref,
    weight_ref,
    angle_ref,
    width_ref,
    rbed_ref,
    local_sem,
    bed,
    lev,
    fields,
    hot,
    found,
    terms,
    spots,
    sums,
    recv,
    weights,
    halo_send,
    halo_recv,
    send_sem,
    recv_sem,
):
    n_lon, n_lat, rows, cols = dims
    owners = n_lon * n_lat
    lon, lat = lax.axis_index("lon"), lax.axis_index("lat")
    me = lon * n_lat + lat
    tall, wide = rows + 2 * PAD_R, cols + 2 * PAD_C
    slot_rows = cell_ref.shape[0]

    barrier = pltpu.get_barrier_semaphore()

    def peer(step):
        other = lax.rem(me + step, owners)
        return {"lon": other // n_lat, "lat": lax.rem(other, n_lat)}

    def greet(step, carry):
        pl.semaphore_signal(barrier, inc=1, device_id=peer(step), device_id_type=MESH)
        return carry

    lax.fori_loop(1, owners, greet, 0, unroll=5)
    middle = (pl.ds(PAD_R, rows), pl.ds(PAD_C, cols))
    pairs = (
        (weight_in, weight_ref),
        (angle_in, angle_ref),
        (bed_ref, bed.at[middle]),
        (cot_ref, lev.at[middle]),
        (cell_in, cell_ref),
        (owner_in, owner_ref),
        (reach_in, reach_ref),
        (width_in, width_ref),
        (rbed_in, rbed_ref),
    )
    loads = [
        pltpu.make_async_copy(source, place, local_sem.at[i])
        for i, (source, place) in enumerate(pairs)
    ]
    for load in loads:
        load.start()
    half = cols // 2
    picks = 2 * rows
    reach_rows = width_ref.shape[0] // 2
    per_owner = 2 * reach_rows
    table = owners * per_owner
    blocks = slot_rows // GROUP

    def mark_reach(number, carry):
        here = pl.ds(pl.multiple_of(number * GROUP, GROUP), GROUP)
        reach = reach_ref[here, :]
        lane = (reach // LANES // reach_rows) * LANES + reach % LANES
        upright = jnp.transpose(lane.astype(jnp.float32)).astype(jnp.int32)
        lane_ids = lax.broadcasted_iota(jnp.int32, (LANES, TABLE), 1)
        for i in range(GROUP):
            spots[number, i * LANES : (i + 1) * LANES, :] = jnp.where(
                lane_ids == upright[:, i : i + 1], 1.0, 0.0
            ).astype(jnp.bfloat16)
        return carry

    pl.semaphore_wait(barrier, owners - 1)

    def span(step, length, pad):
        if step == 0:
            return pl.ds(0, length), pl.ds(pad, length)
        if step > 0:
            return pl.ds(length - pad, pad), pl.ds(0, pad)
        return pl.ds(0, pad), pl.ds(pad + length, pad)

    copies = []
    for d_lon, d_lat in ((1, 0), (-1, 0), (1, 1), (1, -1), (-1, 1), (-1, -1), (0, 1), (0, -1)):
        from_r, to_r = span(d_lat, rows, PAD_R)
        from_c, to_c = span(d_lon, cols, PAD_C)
        target = {
            "lon": lax.rem(lon + d_lon + n_lon, n_lon),
            "lat": lax.rem(lat + d_lat + n_lat, n_lat),
        }
        for source, place in ((bed_ref, bed), (cot_ref, lev)):
            index = len(copies)
            copy = pltpu.make_async_remote_copy(
                src_ref=source.at[from_r, from_c],
                dst_ref=place.at[to_r, to_c],
                send_sem=halo_send.at[index],
                recv_sem=halo_recv.at[index],
                device_id=target,
                device_id_type=MESH,
            )
            copy.start()
            copies.append(copy)

    for load in loads:
        load.wait()
    lax.fori_loop(0, blocks, mark_reach, 0)

    slot = (
        lax.broadcasted_iota(jnp.int32, (slot_rows, LANES), 0) * LANES
        + lax.broadcasted_iota(jnp.int32, (slot_rows, LANES), 1)
    )
    weight = jnp.where(slot < count_ref[0], weight_ref[...], 0.0)
    angle = angle_ref[...]
    weights[0] = weight
    weights[1] = weight * jnp.cos(angle)
    weights[2] = weight * jnp.sin(angle)
    sums[...] = jnp.zeros_like(sums)

    def mark(number, carry):
        here = pl.ds(pl.multiple_of(number * GROUP, GROUP), GROUP)
        deep = cell_ref[here, :] % half
        deep_ids = lax.broadcasted_iota(jnp.int32, (half, LANES), 0)
        for i in range(GROUP):
            at = slice(i * LANES, (i + 1) * LANES)
            hot[number, :, at] = jnp.where(deep_ids == deep[i : i + 1], 1.0, 0.0).astype(
                jnp.bfloat16
            )
        return carry

    lax.fori_loop(0, blocks, mark, 0)

    for copy in copies:
        copy.wait()

    def east(value):
        return pltpu.roll(value, wide - 1, 1)

    def west(value):
        return pltpu.roll(value, 1, 1)

    def north(value):
        return pltpu.roll(value, tall - 1, 0)

    def south(value):
        return pltpu.roll(value, 1, 0)

    row = lat * rows - PAD_R + lax.broadcasted_iota(jnp.int32, (tall, wide), 0)
    open_north = (row >= 0) & (row < n_lat * rows - 1)
    depth = bed[...]
    east_depth = 0.5 * (depth + east(depth))
    north_depth = 0.5 * (depth + north(depth))
    east_keep = east_depth / (east_depth + DRAG_RATE)
    north_keep = jnp.where(open_north, north_depth / (north_depth + DRAG_RATE), 0.0)
    east_gain = WAVE_GAIN * east_keep * east_depth
    north_gain = WAVE_GAIN * north_keep * north_depth
    level = lev[...]
    sum_level = level
    for step in range(STEPS):
        east_mid = east(level) - level
        north_mid = north(level) - level
        if step > 0:
            sum_level = sum_level + level
            east_mid = east_mid + east_adj
            north_mid = north_mid + north_adj
        north_mid = jnp.where(open_north, north_mid, 0.0)
        east_flux = east_gain * east_mid
        north_flux = north_gain * north_mid
        level = level + east_flux - west(east_flux) + north_flux - south(north_flux)
        if step == 0:
            sum_east, sum_north = east_mid, north_mid
        else:
            sum_east, sum_north = sum_east + east_mid, sum_north + north_mid
        if step + 1 < STEPS:
            east_adj = east_keep * east_mid
            north_adj = north_keep * north_mid
    level_out[...] = level[PAD_R : PAD_R + rows, PAD_C : PAD_C + cols]

    for index, value in enumerate((sum_level, sum_east, sum_north)):
        for side in range(2):
            first = PAD_C + side * half
            high, low = split(value[PAD_R : PAD_R + rows, first : first + half])
            place = slice(index * picks + side * rows, index * picks + (side + 1) * rows)
            fields[place, 0:half] = high.astype(jnp.bfloat16)
            fields[place, half : 2 * half] = low.astype(jnp.bfloat16)

    def found_in(number):
        here = hot[number]
        return jnp.dot(
            fields[:, 0:half], here, preferred_element_type=jnp.float32
        ) + jnp.dot(fields[:, half : 2 * half], here, preferred_element_type=jnp.float32)

    def add_terms(number, side):
        here = pl.ds(pl.multiple_of(number * GROUP, GROUP), GROUP)
        cell = cell_ref[here, :]
        pick = ((cell % cols) // half) * rows + cell // cols
        key = owner_ref[here, :] * reach_rows + (reach_ref[here, :] // LANES) % reach_rows
        for_level, for_east, for_north = (weights[i, here, :] for i in range(3))
        pick_ids = lax.broadcasted_iota(jnp.int32, (picks, LANES), 0)
        line_ids = lax.broadcasted_iota(jnp.int32, (table, LANES), 0)
        key_ids = (line_ids // per_owner) * reach_rows + line_ids % reach_rows
        is_flow = (line_ids // reach_rows) % 2 == 1
        for i in range(GROUP):
            at = slice(i * LANES, (i + 1) * LANES)
            mine = pick_ids == pick[i : i + 1]
            value = [
                jnp.sum(
                    jnp.where(mine, found[side, f * picks : (f + 1) * picks, at], 0.0),
                    axis=0,
                    keepdims=True,
                )
                for f in range(3)
            ]
            level_high, level_low = split(for_level[i : i + 1] * value[0])
            flow_high, flow_low = split(
                for_east[i : i + 1] * value[1] + for_north[i : i + 1] * value[2]
            )
            line = key_ids == key[i : i + 1]
            terms[side, 0:table, at] = jnp.where(
                line, jnp.where(is_flow, flow_high, level_high), 0.0
            ).astype(jnp.bfloat16)
            terms[side, table : 2 * table, at] = jnp.where(
                line, jnp.where(is_flow, flow_low, level_low), 0.0
            ).astype(jnp.bfloat16)
        added = jnp.dot(terms[side], spots[number], preferred_element_type=jnp.float32)
        sums[...] += added[0:table] + added[table : 2 * table]

    found[0] = found_in(0)

    def two_blocks(pair, carry):
        for side in range(2):
            found[1 - side] = found_in(2 * pair + side + 1)
            add_terms(2 * pair + side, side)
        return carry

    lax.fori_loop(0, blocks // 2 - 1, two_blocks, 0)
    found[1] = found_in(blocks - 1)
    add_terms(blocks - 2, 0)
    add_terms(blocks - 1, 1)

    def outgoing(step):
        other = lax.rem(me + step, owners)
        return pltpu.make_async_remote_copy(
            src_ref=sums.at[pl.ds(pl.multiple_of(other * per_owner, per_owner), per_owner)],
            dst_ref=recv.at[step],
            send_sem=send_sem.at[step],
            recv_sem=recv_sem.at[step],
            device_id=peer(step),
            device_id_type=MESH,
        )

    def send(step, carry):
        outgoing(step).start()
        return carry

    def take(step, total):
        outgoing(step).wait()
        return total + recv[step]

    lax.fori_loop(1, owners, send, 0, unroll=5)
    own = sums[pl.ds(pl.multiple_of(me * per_owner, per_owner), per_owner), :]
    total = lax.fori_loop(1, owners, take, own, unroll=5)
    level_total = jnp.concatenate(
        [total[0:reach_rows, 0:LANES], total[0:reach_rows, LANES:TABLE]], axis=0
    )
    flow_total = jnp.concatenate(
        [total[reach_rows:per_owner, 0:LANES], total[reach_rows:per_owner, LANES:TABLE]], axis=0
    )
    gwidth_out[...] = rbed_ref[...] * level_total
    gbed_out[...] = width_ref[...] * level_total + rbed_ref[...] * flow_total


def on_device(
    dims,
    bed_depth,
    cotangent,
    sample_cell,
    sample_owner,
    sample_reach,
    sample_weight,
    sample_angle,
    sample_count,
    reach_width,
    reach_bed,
):
    n_lon, n_lat = dims
    rows, cols = bed_depth.shape
    owners = n_lon * n_lat
    tall, wide = rows + 2 * PAD_R, cols + 2 * PAD_C
    slot_rows = sample_cell.shape[0] // LANES
    reach_tiles = reach_width.shape[0] // LANES
    per_owner = reach_tiles
    block = GROUP * LANES
    blocks = slot_rows // GROUP

    def tiled(value):
        return value.reshape(-1, LANES)

    hbm = pl.BlockSpec(memory_space=pltpu.HBM)
    def in_hbm(value):
        return pltpu.with_memory_space_constraint(value, pltpu.HBM)

    vmem = pl.BlockSpec(memory_space=pltpu.VMEM)
    level, gwidth, gbed = pl.pallas_call(
        functools.partial(kernel, (n_lon, n_lat, rows, cols)),
        out_shape=(
            jax.ShapeDtypeStruct((rows, cols), jnp.float32),
            jax.ShapeDtypeStruct((reach_tiles, LANES), jnp.float32),
            jax.ShapeDtypeStruct((reach_tiles, LANES), jnp.float32),
        ),
        in_specs=[hbm] * 7 + [pl.BlockSpec(memory_space=pltpu.SMEM)] + [hbm] * 2,
        out_specs=(vmem, vmem, vmem),
        scratch_shapes=[
            pltpu.VMEM((slot_rows, LANES), jnp.int32),
            pltpu.VMEM((slot_rows, LANES), jnp.int32),
            pltpu.VMEM((slot_rows, LANES), jnp.int32),
            pltpu.VMEM((slot_rows, LANES), jnp.float32),
            pltpu.VMEM((slot_rows, LANES), jnp.float32),
            pltpu.VMEM((reach_tiles, LANES), jnp.float32),
            pltpu.VMEM((reach_tiles, LANES), jnp.float32),
            pltpu.SemaphoreType.DMA((9,)),
            pltpu.VMEM((tall, wide), jnp.float32),
            pltpu.VMEM((tall, wide), jnp.float32),
            pltpu.VMEM((6 * rows, cols), jnp.bfloat16),
            pltpu.VMEM((blocks, cols // 2, block), jnp.bfloat16),
            pltpu.VMEM((2, 6 * rows, block), jnp.float32),
            pltpu.VMEM((2, 2 * owners * per_owner, block), jnp.bfloat16),
            pltpu.VMEM((blocks, block, TABLE), jnp.bfloat16),
            pltpu.VMEM((owners * per_owner, TABLE), jnp.float32),
            pltpu.VMEM((owners, per_owner, TABLE), jnp.float32),
            pltpu.VMEM((3, slot_rows, LANES), jnp.float32),
            pltpu.SemaphoreType.DMA((16,)),
            pltpu.SemaphoreType.DMA((16,)),
            pltpu.SemaphoreType.DMA((owners,)),
            pltpu.SemaphoreType.DMA((owners,)),
        ],
        compiler_params=pltpu.CompilerParams(
            collective_id=0, has_side_effects=True, vmem_limit_bytes=48 << 20
        ),
    )(
        in_hbm(bed_depth),
        in_hbm(cotangent),
        in_hbm(tiled(sample_cell)),
        in_hbm(tiled(sample_owner)),
        in_hbm(tiled(sample_reach)),
        in_hbm(tiled(sample_weight)),
        in_hbm(tiled(sample_angle)),
        sample_count,
        in_hbm(tiled(reach_width)),
        in_hbm(tiled(reach_bed)),
    )
    return level, gwidth.reshape(-1), gbed.reshape(-1)


def solution(mesh):
    flat = P(("lon", "lat"))
    return jax.shard_map(
        functools.partial(on_device, (mesh.shape["lon"], mesh.shape["lat"])),
        mesh=mesh,
        in_specs=(P("lat", "lon"), P(("ens", "lat"), "lon")) + (flat,) * 8,
        out_specs=(P(("ens", "lat"), "lon"), P(("ens", "lon", "lat")), P(("ens", "lon", "lat"))),
        check_vma=False,
    )
```
